32 devices in a mesh: dp: 8 (over z, y), mp: 4 (over x, core).
Axes of the slice: x: 2, y: 2, z: 4, core: 2. Of those that a mesh axis runs over, the one named last changes fastest.
Arguments:
- tokens: bfloat16 [2048, 2048], P('dp'), may hold values from -6 to 6
- lengths: int32 [4], replicated, may hold values from 1 to 1024, 2048 in all
- w_query: float32 [2048, 2048], P('dp', 'mp')
- w_key: float32 [2048, 2048], P('dp', 'mp')
- w_value: float32 [2048, 2048], P('dp', 'mp'), may hold values from -0.125 to 0.125
- w_out: float32 [2048, 2048], P('dp', 'mp'), may hold values from -0.125 to 0.125
- w_gate: float32 [2048, 4096], P('dp', 'mp'), may hold values from -0.125 to 0.125
- w_up: float32 [2048, 4096], P('dp', 'mp'), may hold values from -0.125 to 0.125
- w_down: float32 [4096, 2048], P('dp', 'mp'), may hold values from -0.09375 to 0.09375
Outputs:
- layer_out: bfloat16 [2048, 2048], P(('dp', 'mp'))
The draws below stay inside these ranges and needn't reach their ends.
Inputs may be any that keep to these rules, and one draw needn't show every extreme that they name: Every prompt is 1 to 1024 tokens long and one is exactly 1024; the lengths sum to 2048.
All inputs are finite; a program needn't handle non-finite values.
Results may differ from the reference program's by a relative error of at most 0.02.
The reference program's roundings to bfloat16 on the way count: a program that leaves them out, or rounds other values in their place, can miss the bound.
Values may be sent and summed in bfloat16 or wider, within the bound.
A program may use at most 128 MiB of HBM per device.

```python
import math
import jax
import jax.numpy as jnp
import numpy as np
from jax import lax

D = 2048
FF = 4096
HEAD = 128
PROMPTS = 4
TOK_DEV = 256
HEADS = 16
TOKENS = 2048
REACH = 4
MOST = 1024


def projection_draw(key):
    base_key = jax.random.fold_in(key, 0)
    matrix = jax.random.normal(base_key, (D, D), jnp.float32) * D ** (-0.5)
    return matrix


def draw_w_query(key, part):
    return projection_draw(jax.random.fold_in(key, 11))


def draw_w_key(key, part):
    return projection_draw(jax.random.fold_in(key, 12))


def levels(key, dims, shards, smallest, high):
    factor_of, own = 1.0, jax.random.fold_in(key, 6)
    for axis_at, blocks in shards:
        draws = jnp.exp(jax.random.uniform(jax.random.fold_in(own, axis_at), (blocks,), jnp.float32, smallest / len(shards), high / len(shards)))
        factor_of = factor_of * jnp.repeat(draws, dims[axis_at] // blocks).reshape([-1 if axis == axis_at else 1 for axis in range(len(dims))])
    return factor_of


def split_up(number_of, total, limit, skew):
    portions = [(1 << 20) // math.isqrt(rank ** skew) + 1 for rank in range(2, number_of + 1)]
    surplus, holding = total - limit - (number_of - 1), [1] * (number_of - 1)
    while surplus > 0:
        movable = [i for i in range(number_of - 1) if holding[i] < limit]
        pool, left = sum([portions[i] for i in movable]), surplus
        for i in movable:
            more = min(limit - holding[i], max(1, left * portions[i] // pool), surplus)
            holding[i] = holding[i] + more
            surplus = surplus - more
    return np.array([limit] + holding)


def ragged(own_key, amount, total, limit, slope):
    if amount == 2:
        one = jax.random.randint(own_key, (), max(1, total - limit), min(limit, total - 1) + 1)
        return jnp.stack([one, total - one])
    tallies = jnp.asarray(split_up(amount, total, limit, slope), jnp.int32)
    couples = (amount - 1) // 2
    giver, taker = tallies[1:1 + 2 * couples:2], tallies[2:2 + 2 * couples:2]
    room = jnp.minimum(giver - 1, limit - taker)
    shifted = jax.random.randint(jax.random.fold_in(own_key, 1), (couples,), 0, 1 << 20) % (room + 1)
    tallies = tallies.at[1:1 + 2 * couples:2].set(giver - shifted).at[2:2 + 2 * couples:2].set(taker + shifted)
    return tallies[jax.random.permutation(jax.random.fold_in(own_key, 2), amount)]


def scatter_about(rng, dims, scale, limit, cuts=(), kind=jnp.bfloat16):
    loudness = levels(rng, dims, cuts, -0.22, 0.18) if cuts else 1.0
    array = jax.random.normal(rng, dims, jnp.float32) * scale * loudness
    return jnp.minimum(jnp.maximum(array, -limit), limit).astype(kind)


def setup_inputs(seed: int = 0) -> dict:
    seeds = jax.random.split(jax.random.key(seed), 10)
    tokens = scatter_about(seeds[0], (TOKENS, D), 1.0, 6.0, ((0, 8),))
    lengths = ragged(seeds[1], PROMPTS, TOKENS, MOST, 2).astype(jnp.int32)
    w_query = draw_w_query(jax.random.fold_in(seeds[9], 71), 0)
    w_key = draw_w_key(jax.random.fold_in(seeds[9], 71), 0)
    w_value = scatter_about(seeds[4], (D, D), D ** -0.5, 0.125, ((0, 8), (1, 4)), jnp.float32)
    w_out = scatter_about(seeds[5], (D, D), D ** -0.5, 0.125, ((0, 8), (1, 4)), jnp.float32)
    w_gate = scatter_about(seeds[6], (D, FF), D ** -0.5, 0.125, ((0, 8), (1, 4)), jnp.float32)
    w_up = scatter_about(seeds[7], (D, FF), D ** -0.5, 0.125, ((0, 8), (1, 4)), jnp.float32)
    w_down = scatter_about(seeds[8], (FF, D), FF ** -0.5, 0.09375, ((0, 8), (1, 4)), jnp.float32)
    return dict(tokens=tokens, lengths=lengths, w_query=w_query, w_key=w_key, w_value=w_value, w_out=w_out, w_gate=w_gate, w_up=w_up, w_down=w_down)


epsilon = 1e-05
theta_base = 10000.0

def layer_norm(rows):
    values = rows.astype(jnp.float32)
    centre = lax.optimization_barrier(jnp.mean(values, axis=-1, keepdims=True))
    spread = lax.optimization_barrier(jnp.mean(jnp.square(values - centre), axis=-1, keepdims=True))
    return (values - centre) * lax.rsqrt(spread + epsilon)

def prompt_coords(first, count, lengths):
    where = (first + jnp.arange(count)).astype(jnp.int32)
    ends = jnp.cumsum(lengths).astype(jnp.int32)
    passed = (ends[None, :] <= where[:, None]).astype(jnp.int32)
    prompt = lax.optimization_barrier(jnp.sum(passed, axis=1)).astype(jnp.int32)
    offset = (where - lax.optimization_barrier(jnp.sum(passed * lengths[None, :], axis=1))).astype(jnp.int32)
    prompt = jnp.where(where < 0, -1, prompt).astype(jnp.int32)
    return (prompt, offset, where)

def rotate(values, offset):
    half = values.shape[-1] // 2
    freqs = jnp.power(theta_base, -jnp.arange(half, dtype=jnp.float32) * 2.0 / values.shape[-1])
    angles = offset.astype(jnp.float32)[:, None] * freqs[None, :]
    cosine = jnp.cos(angles)[:, None, :]
    sine = jnp.sin(angles)[:, None, :]
    first_half = values[..., :half]
    second_half = values[..., half:]
    return jnp.concatenate([first_half * cosine - second_half * sine, second_half * cosine + first_half * sine], axis=-1)

def online_step(state, query, keys, values, q_prompt, q_where, k_prompt, k_where):
    accum, total, top = state
    scale = 1.0 / query.shape[-1] ** 0.5
    scores = jnp.einsum('qhd,khd->hqk', query.astype(jnp.float32), keys.astype(jnp.float32)) * scale
    allowed = (q_prompt[:, None] == k_prompt[None, :]) & (k_where[None, :] <= q_where[:, None])
    scores = jnp.where(allowed[None], scores, -jnp.inf)
    new_top = jnp.maximum(top, lax.optimization_barrier(jnp.max(scores, axis=-1, keepdims=True)))
    fade = jnp.exp(top - new_top)
    weights = jnp.exp(scores - new_top)
    probs = weights.astype(jnp.bfloat16)
    product = jnp.einsum('hqk,khd->qhd', probs.astype(jnp.float32), values.astype(jnp.float32))
    accum = accum * jnp.transpose(fade, (1, 0, 2)) + product
    total = total * fade + lax.optimization_barrier(jnp.sum(weights, axis=-1, keepdims=True))
    return (accum, total, new_top)

def reference(tokens, lengths, w_query, w_key, w_value, w_out, w_gate, w_up, w_down):
    half_type = jnp.bfloat16
    normed = layer_norm(tokens).astype(half_type)
    prompt, offset, where = prompt_coords(0, TOKENS, lengths)
    query = jnp.dot(normed, w_query.astype(half_type), preferred_element_type=jnp.float32)
    keys = jnp.dot(normed, w_key.astype(half_type), preferred_element_type=jnp.float32)
    values = jnp.dot(normed, w_value.astype(half_type), preferred_element_type=jnp.float32)
    query = rotate(query.reshape(TOKENS, HEADS, HEAD), offset).astype(half_type)
    keys = rotate(keys.reshape(TOKENS, HEADS, HEAD), offset).astype(half_type)
    values = values.astype(half_type).reshape(TOKENS, HEADS, HEAD)
    margin = REACH * TOK_DEV
    keys_pad = jnp.concatenate([jnp.zeros((margin, HEADS, HEAD), half_type), keys], axis=0)
    values_pad = jnp.concatenate([jnp.zeros((margin, HEADS, HEAD), half_type), values], axis=0)
    k_prompt_pad, k_offset_pad, k_where_pad = prompt_coords(-margin, TOKENS + margin, lengths)

    def one_block(block):
        first = (block * TOK_DEV).astype(jnp.int32)
        q_block = lax.dynamic_slice_in_dim(query, first, TOK_DEV, 0)
        qp = lax.dynamic_slice_in_dim(prompt, first, TOK_DEV, 0)
        qw = lax.dynamic_slice_in_dim(where, first, TOK_DEV, 0)
        state = (jnp.zeros((TOK_DEV, HEADS, HEAD), jnp.float32), jnp.zeros((HEADS, TOK_DEV, 1), jnp.float32), jnp.full((HEADS, TOK_DEV, 1), -jnp.inf, jnp.float32))

        def slot_step(slot, state):
            start = (first + margin - slot * TOK_DEV).astype(jnp.int32)
            k_block = lax.dynamic_slice_in_dim(keys_pad, start, TOK_DEV, 0)
            v_block = lax.dynamic_slice_in_dim(values_pad, start, TOK_DEV, 0)
            kp = lax.dynamic_slice_in_dim(k_prompt_pad, start, TOK_DEV, 0)
            kw = lax.dynamic_slice_in_dim(k_where_pad, start, TOK_DEV, 0)
            return online_step(state, q_block, k_block, v_block, qp, qw, kp, kw)
        accum, total, top = lax.fori_loop(0, REACH + 1, slot_step, state)
        return (accum / jnp.transpose(total, (1, 0, 2))).astype(half_type)
    context = lax.map(one_block, jnp.arange(TOKENS // TOK_DEV, dtype=jnp.int32)).reshape(TOKENS, D)
    attended = jnp.dot(context, w_out.astype(half_type), preferred_element_type=jnp.float32)
    mixed = (tokens.astype(jnp.float32) + attended).astype(half_type)
    normed_two = layer_norm(mixed).astype(half_type)
    gate = jnp.dot(normed_two, w_gate.astype(half_type), preferred_element_type=jnp.float32)
    upper = jnp.dot(normed_two, w_up.astype(half_type), preferred_element_type=jnp.float32)
    hidden = (jax.nn.silu(gate) * upper).astype(half_type)
    mlp_sum = jnp.dot(hidden, w_down.astype(half_type), preferred_element_type=jnp.float32)
    return (mixed.astype(jnp.float32) + mlp_sum).astype(half_type)
```

```python
import jax
import jax.numpy as jnp
from jax import lax
from jax.sharding import PartitionSpec as P

HEAD = 128


epsilon = 1e-05
theta_base = 10000.0


def passed_along(value, axis, steps):
    count = lax.axis_size(axis)
    initial, last = (max(0, -steps), min(count, count - steps))
    return lax.ppermute(value, axis, [(source, source + steps) for source in range(initial, last)])


def layer_norm(rows):
    values = rows.astype(jnp.float32)
    centre = jnp.mean(values, axis=-1, keepdims=True)
    spread = jnp.mean(jnp.square(values - centre), axis=-1, keepdims=True)
    return (values - centre) * lax.rsqrt(spread + epsilon)


def prompt_coords(first, count, lengths):
    where = first + jnp.arange(count)
    upto = jnp.arange(lengths.shape[0])
    ends = jnp.sum(jnp.where(upto[None, :] <= upto[:, None], lengths[None, :], 0), axis=1)
    passed = (ends[None, :] <= where[:, None]).astype(jnp.int32)
    prompt = jnp.sum(passed, axis=1)
    offset = where - jnp.sum(passed * lengths[None, :], axis=1)
    prompt = jnp.where(where < 0, -1, prompt)
    return (prompt, offset, where)


def rotate(values, offset):
    half = values.shape[-1] // 2
    freqs = jnp.power(theta_base, -jnp.arange(half, dtype=jnp.float32) * 2.0 / values.shape[-1])
    angles = offset.astype(jnp.float32)[:, None] * freqs[None, :]
    cosine = jnp.cos(angles)[:, None, :]
    sine = jnp.sin(angles)[:, None, :]
    first_half = values[..., :half]
    second_half = values[..., half:]
    return jnp.concatenate(
        [first_half * cosine - second_half * sine, second_half * cosine + first_half * sine],
        axis=-1,
    )


def on_device(tokens, lengths, w_query, w_key, w_value, w_out, w_gate, w_up, w_down):
    half_type = jnp.bfloat16
    rows = tokens.shape[0]
    narrow = w_query.shape[1]
    heads_dev = narrow // HEAD
    dp_index = lax.axis_index("dp")
    mp_index = lax.axis_index("mp")
    reach = lax.axis_size("dp") // 2
    normed = layer_norm(tokens).astype(half_type)
    packed_in = jnp.concatenate([w.astype(half_type) for w in (w_query, w_key, w_value)], axis=1)
    server_in = lax.all_gather(packed_in, "dp", axis=0, tiled=True)
    packed_mid = jnp.concatenate([w.astype(half_type) for w in (w_out, w_gate, w_up)], axis=1)
    down = w_down.astype(half_type)
    server_in, packed_mid, down = lax.optimization_barrier((server_in, packed_mid, down))
    server_mid = lax.all_gather(packed_mid, "dp", axis=0, tiled=True)
    server_mid, down = lax.optimization_barrier((server_mid, down))
    server_down = lax.all_gather(down, "dp", axis=0, tiled=True)
    joined = jnp.dot(normed, server_in, preferred_element_type=jnp.float32)
    q_prompt, q_offset, q_where = prompt_coords(dp_index * rows, rows, lengths)
    shaped = joined.reshape(rows, 3, heads_dev, HEAD)
    query = rotate(shaped[:, 0], q_offset).astype(half_type)
    keys = rotate(shaped[:, 1], q_offset).astype(half_type)
    values = shaped[:, 2].astype(half_type)
    own_first = dp_index * rows
    own_pair = jnp.stack((keys, values))
    scale = 1.0 / HEAD**0.5

    def online_step(state, pair, first):
        accum, total, top = state
        k_prompt, k_offset, k_where = prompt_coords(first, rows, lengths)
        scores = (
            jnp.einsum("qhd,khd->hqk", query, pair[0], preferred_element_type=jnp.float32) * scale
        )
        allowed = (q_prompt[:, None] == k_prompt[None, :]) & (k_where[None, :] <= q_where[:, None])
        scores = jnp.where(allowed[None], scores, -jnp.inf)
        new_top = jnp.maximum(top, jnp.max(scores, axis=-1, keepdims=True))
        fade = jnp.exp(top - new_top)
        weights = jnp.exp(scores - new_top)
        probs = weights.astype(half_type)
        product = jnp.einsum("hqk,khd->qhd", probs, pair[1], preferred_element_type=jnp.float32)
        accum = accum * jnp.transpose(fade, (1, 0, 2)) + product
        total = total * fade + jnp.sum(weights, axis=-1, keepdims=True)
        return (accum, total, new_top)

    start_state = (
        jnp.zeros((rows, heads_dev, HEAD), jnp.float32),
        jnp.zeros((heads_dev, rows, 1), jnp.float32),
        jnp.full((heads_dev, rows, 1), -jnp.inf, jnp.float32),
    )
    state = online_step(start_state, own_pair, own_first)

    def relay_step(hop, carry):
        carried, running = carry
        carried = passed_along(carried, "dp", 1)
        first = own_first - (hop + 1) * rows
        return (carried, online_step(running, carried, first))

    unused, state = lax.fori_loop(0, reach, relay_step, (own_pair, state))
    accum, total, top = state
    context = (accum / jnp.transpose(total, (1, 0, 2))).astype(half_type).reshape(rows, narrow)
    all_heads = lax.all_gather(context, "mp", axis=1, tiled=True)
    attended = jnp.dot(all_heads, server_mid[:, :narrow], preferred_element_type=jnp.float32)
    own_columns = lax.dynamic_slice_in_dim(tokens, mp_index * narrow, narrow, 1)
    own_mixed = (own_columns.astype(jnp.float32) + attended).astype(half_type)
    mixed = lax.all_gather(own_mixed, "mp", axis=1, tiled=True)
    normed_two = layer_norm(mixed).astype(half_type)
    units = w_gate.shape[1]
    gate_up = jnp.dot(normed_two, server_mid[:, narrow:], preferred_element_type=jnp.float32)
    hidden = (jax.nn.silu(gate_up[:, :units]) * gate_up[:, units:]).astype(half_type)
    all_hidden = lax.all_gather(hidden, "mp", axis=1, tiled=True)
    product = jnp.dot(all_hidden, server_down, preferred_element_type=jnp.float32)
    own_out = (own_mixed.astype(jnp.float32) + product).astype(half_type)
    return lax.all_to_all(own_out, "mp", split_axis=0, concat_axis=1, tiled=True)


def solution(mesh):
    in_specs = (
        P("dp", None),
        P(),
        P("dp", "mp"),
        P("dp", "mp"),
        P("dp", "mp"),
        P("dp", "mp"),
        P("dp", "mp"),
        P("dp", "mp"),
        P("dp", "mp"),
    )
    out_specs = P(("dp", "mp"), None)
    return jax.shard_map(
        on_device, mesh=mesh, in_specs=in_specs, out_specs=out_specs, check_vma=False
    )
```

```python
import functools

import jax
import jax.numpy as jnp
from jax import lax
from jax.experimental import pallas as pl
from jax.experimental.pallas import tpu as pltpu
from jax.sharding import PartitionSpec as P

HEAD = 128


epsilon = 1e-05
theta_base = 10000.0


def passed_along(value, axis, steps):
    count = lax.axis_size(axis)
    initial, last = (max(0, -steps), min(count, count - steps))
    return lax.ppermute(value, axis, [(source, source + steps) for source in range(initial, last)])


def layer_norm(rows):
    values = rows.astype(jnp.float32)
    centre = jnp.mean(values, axis=-1, keepdims=True)
    spread = jnp.mean(jnp.square(values - centre), axis=-1, keepdims=True)
    return (values - centre) * lax.rsqrt(spread + epsilon)


def prompt_coords(first, count, lengths):
    where = first + jnp.arange(count)
    upto = jnp.arange(lengths.shape[0])
    ends = jnp.sum(jnp.where(upto[None, :] <= upto[:, None], lengths[None, :], 0), axis=1)
    passed = (ends[None, :] <= where[:, None]).astype(jnp.int32)
    prompt = jnp.sum(passed, axis=1)
    offset = where - jnp.sum(passed * lengths[None, :], axis=1)
    prompt = jnp.where(where < 0, -1, prompt)
    return (prompt, offset, where)


def rotate(values, offset):
    half = values.shape[-1] // 2
    freqs = jnp.power(theta_base, -jnp.arange(half, dtype=jnp.float32) * 2.0 / values.shape[-1])
    angles = offset.astype(jnp.float32)[:, None] * freqs[None, :]
    cosine = jnp.cos(angles)[:, None, :]
    sine = jnp.sin(angles)[:, None, :]
    first_half = values[..., :half]
    second_half = values[..., half:]
    return jnp.concatenate(
        [first_half * cosine - second_half * sine, second_half * cosine + first_half * sine],
        axis=-1,
    )


def on_device(tokens, lengths, w_query, w_key, w_value, w_out, w_gate, w_up, w_down):
    half_type = jnp.bfloat16
    rows = tokens.shape[0]
    narrow = w_query.shape[1]
    heads_dev = narrow // HEAD
    dp_index = lax.axis_index("dp")
    mp_index = lax.axis_index("mp")
    reach = lax.axis_size("dp") // 2
    normed = layer_norm(tokens).astype(half_type)
    packed_in = jnp.concatenate([w.astype(half_type) for w in (w_query, w_key, w_value)], axis=1)
    server_in = lax.all_gather(packed_in, "dp", axis=0, tiled=True)
    packed_mid = jnp.concatenate([w.astype(half_type) for w in (w_out, w_gate, w_up)], axis=1)
    down = w_down.astype(half_type)
    server_in, packed_mid, down = lax.optimization_barrier((server_in, packed_mid, down))
    server_mid = lax.all_gather(packed_mid, "dp", axis=0, tiled=True)
    server_mid, down = lax.optimization_barrier((server_mid, down))
    server_down = lax.all_gather(down, "dp", axis=0, tiled=True)
    joined = jnp.dot(normed, server_in, preferred_element_type=jnp.float32)
    q_prompt, q_offset, q_where = prompt_coords(dp_index * rows, rows, lengths)
    shaped = joined.reshape(rows, 3, heads_dev, HEAD)
    query = rotate(shaped[:, 0], q_offset).astype(half_type)
    keys = rotate(shaped[:, 1], q_offset).astype(half_type)
    values = shaped[:, 2].astype(half_type)
    own_first = dp_index * rows
    own_pair = jnp.stack((keys, values))
    scale = 1.0 / HEAD**0.5

    def online_step(state, pair, first):
        accum, total, top = state
        k_prompt, k_offset, k_where = prompt_coords(first, rows, lengths)
        scores = (
            jnp.einsum("qhd,khd->hqk", query, pair[0], preferred_element_type=jnp.float32) * scale
        )
        allowed = (q_prompt[:, None] == k_prompt[None, :]) & (k_where[None, :] <= q_where[:, None])
        scores = jnp.where(allowed[None], scores, -jnp.inf)
        new_top = jnp.maximum(top, jnp.max(scores, axis=-1, keepdims=True))
        fade = jnp.exp(top - new_top)
        weights = jnp.exp(scores - new_top)
        probs = weights.astype(half_type)
        product = jnp.einsum("hqk,khd->qhd", probs, pair[1], preferred_element_type=jnp.float32)
        accum = accum * jnp.transpose(fade, (1, 0, 2)) + product
        total = total * fade + jnp.sum(weights, axis=-1, keepdims=True)
        return (accum, total, new_top)

    start_state = (
        jnp.zeros((rows, heads_dev, HEAD), jnp.float32),
        jnp.zeros((heads_dev, rows, 1), jnp.float32),
        jnp.full((heads_dev, rows, 1), -jnp.inf, jnp.float32),
    )
    state = online_step(start_state, own_pair, own_first)

    def relay_step(hop, carry):
        carried, running = carry
        carried = passed_along(carried, "dp", 1)
        first = own_first - (hop + 1) * rows
        return (carried, online_step(running, carried, first))

    unused, state = lax.fori_loop(0, reach, relay_step, (own_pair, state))
    accum, total, top = state
    context = (accum / jnp.transpose(total, (1, 0, 2))).astype(half_type).reshape(rows, narrow)
    all_heads = lax.all_gather(context, "mp", axis=1, tiled=True)
    attended = jnp.dot(all_heads, server_mid[:, :narrow], preferred_element_type=jnp.float32)
    own_columns = lax.dynamic_slice_in_dim(tokens, mp_index * narrow, narrow, 1)
    own_mixed = (own_columns.astype(jnp.float32) + attended).astype(half_type)
    mixed = lax.all_gather(own_mixed, "mp", axis=1, tiled=True)
    normed_two = layer_norm(mixed).astype(half_type)
    units = w_gate.shape[1]
    gate_up = jnp.dot(normed_two, server_mid[:, narrow:], preferred_element_type=jnp.float32)
    hidden = (jax.nn.silu(gate_up[:, :units]) * gate_up[:, units:]).astype(half_type)
    all_hidden = lax.all_gather(hidden, "mp", axis=1, tiled=True)
    product = jnp.dot(all_hidden, server_down, preferred_element_type=jnp.float32)
    own_out = (own_mixed.astype(jnp.float32) + product).astype(half_type)
    return lax.all_to_all(own_out, "mp", split_axis=0, concat_axis=1, tiled=True)


def place():
    dp_index, mp_index = lax.axis_index("dp"), lax.axis_index("mp")
    return dp_index // 2, dp_index % 2, mp_index // 2, mp_index % 2


def device(z, y, x, c):
    return (2 * z + y, 2 * x + c)


def remote(source, target, send, receive, where):
    return pltpu.make_async_remote_copy(
        src_ref=source,
        dst_ref=target,
        send_sem=send,
        recv_sem=receive,
        device_id=where,
        device_id_type=pl.DeviceIdType.MESH,
    )


def greet(peers):
    barrier = pltpu.get_barrier_semaphore()
    for peer in peers:
        pl.semaphore_signal(barrier, inc=1, device_id=peer, device_id_type=pl.DeviceIdType.MESH)
    pl.semaphore_wait(barrier, len(peers))


def plane_peers(z, y, x, c):
    return [device(z, y, 1 - x, c), device(z, 1 - y, x, c), device(z, 1 - y, 1 - x, c)]


def column_peers(z, y, x, c):
    steps = [(k, f) for k in range(4) for f in range(2) if k or f]
    return [(k, f, device((z + k) % 4, y, x, (c + f) % 2)) for k, f in steps]


def regroup_kernel(
    in_ref, mid_ref, out_ref, down_ref, rows_ref,
    in_all, mid_all, out_all, down_all, rows_all,
    column_send, column_recv, plane_send, plane_recv,
    part_send, part_recv, fan_send, fan_recv, local_sem,
):
    z, y, x, c = place()
    own = 2 * z + y
    plane = plane_peers(z, y, x, c)
    greet([peer for _, _, peer in column_peers(z, y, x, c)] + plane)
    width = out_ref.shape[-1]

    def columns(mp):
        return pl.ds(pl.multiple_of(mp * width, width), width)

    packs = ((in_ref, in_all), (mid_ref, mid_all))
    locals_ = []
    for i, (source, target) in enumerate(packs):
        locals_.append(pltpu.make_async_copy(source.at[z], target.at[x, own], local_sem.at[i]))
    locals_.append(pltpu.make_async_copy(rows_ref, rows_all.at[z], local_sem.at[2]))
    for copy in locals_:
        copy.start()
    sends = []

    def column_copy(i, k):
        to = (z + k) % 4
        source, target = packs[i] if i < 2 else (rows_ref, rows_all)
        source = source.at[to] if i < 2 else source
        target = target.at[x, own] if i < 2 else target.at[z]
        return remote(source, target, column_send.at[i, k], column_recv.at[i, k], device(to, y, x, c))

    halves = ((out_ref, out_all), (down_ref, down_all))
    hub = y == z // 2

    def part_copy(i, hf):
        source, target = halves[i]
        slot = (z // 2) * 2 + c
        return (
            source.at[hf],
            target.at[z // 2, :, columns(2 * x + c)],
            part_send.at[i, hf],
            part_recv.at[i, slot],
        )

    def is_self(hf):
        return (2 * y + hf == z) & (z % 2 == c)

    for k in (1, 3, 2):
        copy = column_copy(0, k)
        copy.start()
        sends.append(copy)
    for k in (1, 3, 2):
        copy = column_copy(2, k)
        copy.start()
        sends.append(copy)
    for i in range(2):
        for hf in range(2):
            source, target, send, receive = part_copy(i, hf)

            @pl.when(is_self(hf))
            def _():
                pltpu.make_async_copy(source, target, receive).start()

            @pl.when(jnp.logical_not(is_self(hf)))
            def _():
                remote(source, target, send, receive, device(2 * y + hf, y, x, z % 2)).start()
    for k in (1, 3, 2):
        copy = column_copy(1, k)
        copy.start()
        sends.append(copy)

    def fan_copies(i, k):
        block = packs[i][1].at[x, 2 * ((z + 4 - k) % 4) + y]
        return [
            remote(block, block, plane_send.at[i, k, f], plane_recv.at[i, k, f], peer)
            for f, peer in enumerate(plane)
        ]

    def part_block(i, p):
        return halves[i][1].at[p // 2, :, columns(2 * x + p % 2)]

    def part_fan(i, p):
        block = part_block(i, p)
        return [
            remote(block, block, fan_send.at[i, p, f], fan_recv.at[i, p, f], peer)
            for f, peer in enumerate(plane)
        ]

    def forward(i):
        for k in (0, 1, 3, 2):
            if k == 0:
                locals_[i].wait()
            else:
                column_copy(i, k).wait_recv()
            for copy in fan_copies(i, k):
                copy.start()

    forward(0)

    @pl.when(hub)
    def _():
        for i in range(2):
            for p in range(4):
                block = part_block(i, p)
                pltpu.make_async_copy(block, block, part_recv.at[i, p]).wait()
                for copy in part_fan(i, p):
                    copy.start()

    forward(1)
    locals_[2].wait()
    for k in (1, 3, 2):
        column_copy(2, k).wait_recv()
    for copy in sends:
        copy.wait_send()
    for i in range(2):
        for hf in range(2):
            source, target, send, receive = part_copy(i, hf)

            @pl.when(jnp.logical_not(is_self(hf)))
            def _():
                remote(source, target, send, receive, device(2 * y + hf, y, x, z % 2)).wait_send()
        for k in range(4):
            for copy in fan_copies(i, k):
                copy.wait()

    @pl.when(hub)
    def _():
        for i in range(2):
            for p in range(4):
                for copy in part_fan(i, p):
                    copy.wait_send()
                part_fan(i, p)[0].wait_recv()

    @pl.when(jnp.logical_not(hub))
    def _():
        for i in range(2):
            for p in range(4):
                for copy in part_fan(i, p)[1:]:
                    copy.wait_recv()


def any_spec():
    return pl.BlockSpec(memory_space=pl.ANY)


def regroup(*arrays):
    packed_in, packed_mid, out, down, rows = arrays
    half_type = jnp.bfloat16
    depth, cols_in = packed_in.shape[1:]
    cols_mid = packed_mid.shape[2]
    shapes = (
        (2, 8, depth, cols_in),
        (2, 8, depth, cols_mid),
        (2, out.shape[1], 4 * out.shape[2]),
        (2, down.shape[1], 4 * down.shape[2]),
        (4, *rows.shape),
    )
    dma = pltpu.SemaphoreType.DMA
    return pl.pallas_call(
        regroup_kernel,
        out_shape=[jax.ShapeDtypeStruct(shape, half_type) for shape in shapes],
        in_specs=[any_spec()] * 5,
        out_specs=[any_spec()] * 5,
        scratch_shapes=[
            dma((3, 4)), dma((3, 4)), dma((2, 4, 3)), dma((2, 4, 3)),
            dma((2, 2)), dma((2, 4)), dma((2, 4, 3)), dma((2, 4, 3)), dma((3,)),
        ],
        compiler_params=pltpu.CompilerParams(collective_id=0, has_side_effects=True, vmem_limit_bytes=1 << 20),
    )(*arrays)


def plane_kernel(block_ref, all_ref, send, receive, local_sem):
    z, y, x, c = place()
    peers = plane_peers(z, y, x, c)
    greet(peers)
    target = all_ref.at[2 * x + y]
    copies = [remote(block_ref, target, send.at[f], receive.at[f], p) for f, p in enumerate(peers)]
    own = pltpu.make_async_copy(block_ref, target, local_sem)
    for copy in copies:
        copy.start()
    own.start()
    own.wait()
    for copy in copies:
        copy.wait()


def plane_gather(block):
    dma = pltpu.SemaphoreType.DMA
    return pl.pallas_call(
        plane_kernel,
        out_shape=jax.ShapeDtypeStruct((4, *block.shape), block.dtype),
        in_specs=[any_spec()],
        out_specs=any_spec(),
        scratch_shapes=[dma((3,)), dma((3,)), dma(())],
        compiler_params=pltpu.CompilerParams(collective_id=1, has_side_effects=True, vmem_limit_bytes=1 << 20),
    )(block)


def column_kernel(split, block_ref, all_ref, send, receive, local_sem):
    z, y, x, c = place()
    peers = column_peers(z, y, x, c)
    greet([peer for _, _, peer in peers])
    target = all_ref.at[2 * z + c]
    copies = []
    for k, f, peer in peers:
        source = block_ref.at[2 * ((z + k) % 4) + (c + f) % 2] if split else block_ref
        copies.append(remote(source, target, send.at[k, f], receive.at[k, f], peer))
    for copy in copies:
        copy.start()
    own = pltpu.make_async_copy(block_ref.at[2 * z + c] if split else block_ref, target, local_sem)
    own.start()
    own.wait()
    for copy in copies:
        copy.wait()


def column_exchange(block, split, number):
    dma = pltpu.SemaphoreType.DMA
    shape = block.shape if split else (8, *block.shape)
    return pl.pallas_call(
        functools.partial(column_kernel, split),
        out_shape=jax.ShapeDtypeStruct(shape, block.dtype),
        in_specs=[any_spec()],
        out_specs=any_spec(),
        scratch_shapes=[dma((4, 2)), dma((4, 2)), dma(())],
        compiler_params=pltpu.CompilerParams(collective_id=number, has_side_effects=True, vmem_limit_bytes=1 << 20),
    )(block)


def prompt_at(where, lengths):
    upto = jnp.arange(lengths.shape[0])
    ends = jnp.sum(jnp.where(upto[None, :] <= upto[:, None], lengths[None, :], 0), axis=1)
    passed = (ends[None, :] <= where[:, None]).astype(jnp.int32)
    return jnp.sum(passed, axis=1), where - jnp.sum(passed * lengths[None, :], axis=1)


def regrouped(tokens, lengths, w_query, w_key, w_value, w_out, w_gate, w_up, w_down):
    half_type = jnp.bfloat16
    z, y, x, c = place()
    rows, width = tokens.shape
    depth, narrow = w_query.shape
    units = w_gate.shape[1] // 4
    slab = rows // 4

    def pieces(weight):
        return weight.astype(half_type).reshape(weight.shape[0], 4, -1)

    packed_in = jnp.concatenate([pieces(w) for w in (w_query, w_key, w_value)], axis=2).transpose(1, 0, 2)
    packed_mid = jnp.concatenate([pieces(w) for w in (w_gate, w_up)], axis=2).transpose(1, 0, 2)
    out = w_out.astype(half_type).reshape(2, -1, narrow)
    down = w_down.astype(half_type).reshape(2, -1, narrow)
    chip_rows = lax.dynamic_slice_in_dim(tokens, x * 2 * slab, 2 * slab, 0)
    normed = layer_norm(chip_rows).astype(half_type)
    server_in, server_mid, server_out, server_down, normed = regroup(packed_in, packed_mid, out, down, normed)
    count = 8 * slab
    normed = normed.reshape(count, width)
    server_in = server_in.reshape(2, width, 3 * HEAD)
    server_mid = server_mid.reshape(2, width, 2 * units)
    where = (
        jnp.arange(4)[:, None] * (2 * rows) + jnp.arange(2 * slab)[None, :]
    ).reshape(-1)
    q_where = where + y * rows + x * (2 * slab)
    q_prompt, q_offset = prompt_at(q_where, lengths)
    corner = jnp.arange(4)
    k_where = (((corner % 2) * rows + (corner // 2) * (2 * slab))[:, None] + where[None, :]).reshape(-1)
    k_prompt, _ = prompt_at(k_where, lengths)
    joined = [jnp.dot(normed, server_in[i], preferred_element_type=jnp.float32) for i in range(2)]
    query = rotate(jnp.stack([j[:, :HEAD] for j in joined], axis=1), q_offset).astype(half_type)
    keys = rotate(jnp.stack([j[:, HEAD : 2 * HEAD] for j in joined], axis=1), q_offset).astype(half_type)
    block = jnp.concatenate(
        [keys.reshape(count, -1)] + [j[:, 2 * HEAD :].astype(half_type) for j in joined], axis=1
    )
    pairs = plane_gather(block).reshape(4 * count, 4, HEAD)
    allowed = (q_prompt[:, None] == k_prompt[None, :]) & (k_where[None, :] <= q_where[:, None])
    scale = 1.0 / HEAD**0.5
    scores = jnp.einsum("qhd,khd->hqk", query, pairs[:, :2], preferred_element_type=jnp.float32) * scale
    scores = jnp.where(allowed[None], scores, -jnp.inf)
    weights = jnp.exp(scores - jnp.max(scores, axis=-1, keepdims=True))
    total = jnp.sum(weights, axis=-1)
    accum = jnp.einsum("hqk,khd->qhd", weights.astype(half_type), pairs[:, 2:], preferred_element_type=jnp.float32)
    context = (accum / total.T[:, :, None]).astype(half_type).reshape(count, 2 * HEAD)
    partial = jnp.dot(context, server_out.reshape(2 * HEAD, width), preferred_element_type=jnp.float32)
    shares = column_exchange(partial.astype(half_type).reshape(8, slab, width), True, 2)
    attended = jnp.sum(shares.astype(jnp.float32), axis=0)
    own_rows = lax.dynamic_slice_in_dim(tokens, (2 * x + c) * slab, slab, 0)
    mixed = (own_rows.astype(jnp.float32) + attended).astype(half_type)
    normed_two = column_exchange(layer_norm(mixed).astype(half_type), False, 3).reshape(count, width)
    hidden = []
    for i in range(2):
        gate_up = jnp.dot(normed_two, server_mid[i], preferred_element_type=jnp.float32)
        hidden.append((jax.nn.silu(gate_up[:, :units]) * gate_up[:, units:]).astype(half_type))
    hidden = jnp.concatenate(hidden, axis=1)
    product = jnp.dot(hidden, server_down.reshape(2 * units, width), preferred_element_type=jnp.float32)
    shares = column_exchange(product.astype(half_type).reshape(8, slab, width), True, 2)
    return (mixed.astype(jnp.float32) + jnp.sum(shares.astype(jnp.float32), axis=0)).astype(half_type)


def solution(mesh):
    in_specs = (
        P("dp", None),
        P(),
        P("dp", "mp"),
        P("dp", "mp"),
        P("dp", "mp"),
        P("dp", "mp"),
        P("dp", "mp"),
        P("dp", "mp"),
        P("dp", "mp"),
    )
    out_specs = P(("dp", "mp"), None)
    fits = mesh.shape["dp"] == 8 and mesh.shape["mp"] == 4
    return jax.shard_map(
        regrouped if fits else on_device, mesh=mesh, in_specs=in_specs, out_specs=out_specs, check_vma=False
    )
```

```python
import functools

import jax
import jax.numpy as jnp
from jax import lax
from jax.experimental import pallas as pl
from jax.experimental.pallas import tpu as pltpu
from jax.sharding import PartitionSpec as P

HEAD = 128


epsilon = 1e-05
theta_base = 10000.0


def passed_along(value, axis, steps):
    count = lax.axis_size(axis)
    initial, last = (max(0, -steps), min(count, count - steps))
    return lax.ppermute(value, axis, [(source, source + steps) for source in range(initial, last)])


def layer_norm(rows):
    values = rows.astype(jnp.float32)
    centre = jnp.mean(values, axis=-1, keepdims=True)
    spread = jnp.mean(jnp.square(values - centre), axis=-1, keepdims=True)
    return (values - centre) * lax.rsqrt(spread + epsilon)


def prompt_coords(first, count, lengths):
    where = first + jnp.arange(count)
    upto = jnp.arange(lengths.shape[0])
    ends = jnp.sum(jnp.where(upto[None, :] <= upto[:, None], lengths[None, :], 0), axis=1)
    passed = (ends[None, :] <= where[:, None]).astype(jnp.int32)
    prompt = jnp.sum(passed, axis=1)
    offset = where - jnp.sum(passed * lengths[None, :], axis=1)
    prompt = jnp.where(where < 0, -1, prompt)
    return (prompt, offset, where)


def rotate(values, offset):
    half = values.shape[-1] // 2
    freqs = jnp.power(theta_base, -jnp.arange(half, dtype=jnp.float32) * 2.0 / values.shape[-1])
    angles = offset.astype(jnp.float32)[:, None] * freqs[None, :]
    cosine = jnp.cos(angles)[:, None, :]
    sine = jnp.sin(angles)[:, None, :]
    first_half = values[..., :half]
    second_half = values[..., half:]
    return jnp.concatenate(
        [first_half * cosine - second_half * sine, second_half * cosine + first_half * sine],
        axis=-1,
    )


def on_device(tokens, lengths, w_query, w_key, w_value, w_out, w_gate, w_up, w_down):
    half_type = jnp.bfloat16
    rows = tokens.shape[0]
    narrow = w_query.shape[1]
    heads_dev = narrow // HEAD
    dp_index = lax.axis_index("dp")
    mp_index = lax.axis_index("mp")
    reach = lax.axis_size("dp") // 2
    normed = layer_norm(tokens).astype(half_type)
    packed_in = jnp.concatenate([w.astype(half_type) for w in (w_query, w_key, w_value)], axis=1)
    server_in = lax.all_gather(packed_in, "dp", axis=0, tiled=True)
    packed_mid = jnp.concatenate([w.astype(half_type) for w in (w_out, w_gate, w_up)], axis=1)
    down = w_down.astype(half_type)
    server_in, packed_mid, down = lax.optimization_barrier((server_in, packed_mid, down))
    server_mid = lax.all_gather(packed_mid, "dp", axis=0, tiled=True)
    server_mid, down = lax.optimization_barrier((server_mid, down))
    server_down = lax.all_gather(down, "dp", axis=0, tiled=True)
    joined = jnp.dot(normed, server_in, preferred_element_type=jnp.float32)
    q_prompt, q_offset, q_where = prompt_coords(dp_index * rows, rows, lengths)
    shaped = joined.reshape(rows, 3, heads_dev, HEAD)
    query = rotate(shaped[:, 0], q_offset).astype(half_type)
    keys = rotate(shaped[:, 1], q_offset).astype(half_type)
    values = shaped[:, 2].astype(half_type)
    own_first = dp_index * rows
    own_pair = jnp.stack((keys, values))
    scale = 1.0 / HEAD**0.5

    def online_step(state, pair, first):
        accum, total, top = state
        k_prompt, k_offset, k_where = prompt_coords(first, rows, lengths)
        scores = (
            jnp.einsum("qhd,khd->hqk", query, pair[0], preferred_element_type=jnp.float32) * scale
        )
        allowed = (q_prompt[:, None] == k_prompt[None, :]) & (k_where[None, :] <= q_where[:, None])
        scores = jnp.where(allowed[None], scores, -jnp.inf)
        new_top = jnp.maximum(top, jnp.max(scores, axis=-1, keepdims=True))
        fade = jnp.exp(top - new_top)
        weights = jnp.exp(scores - new_top)
        probs = weights.astype(half_type)
        product = jnp.einsum("hqk,khd->qhd", probs, pair[1], preferred_element_type=jnp.float32)
        accum = accum * jnp.transpose(fade, (1, 0, 2)) + product
        total = total * fade + jnp.sum(weights, axis=-1, keepdims=True)
        return (accum, total, new_top)

    start_state = (
        jnp.zeros((rows, heads_dev, HEAD), jnp.float32),
        jnp.zeros((heads_dev, rows, 1), jnp.float32),
        jnp.full((heads_dev, rows, 1), -jnp.inf, jnp.float32),
    )
    state = online_step(start_state, own_pair, own_first)

    def relay_step(hop, carry):
        carried, running = carry
        carried = passed_along(carried, "dp", 1)
        first = own_first - (hop + 1) * rows
        return (carried, online_step(running, carried, first))

    unused, state = lax.fori_loop(0, reach, relay_step, (own_pair, state))
    accum, total, top = state
    context = (accum / jnp.transpose(total, (1, 0, 2))).astype(half_type).reshape(rows, narrow)
    all_heads = lax.all_gather(context, "mp", axis=1, tiled=True)
    attended = jnp.dot(all_heads, server_mid[:, :narrow], preferred_element_type=jnp.float32)
    own_columns = lax.dynamic_slice_in_dim(tokens, mp_index * narrow, narrow, 1)
    own_mixed = (own_columns.astype(jnp.float32) + attended).astype(half_type)
    mixed = lax.all_gather(own_mixed, "mp", axis=1, tiled=True)
    normed_two = layer_norm(mixed).astype(half_type)
    units = w_gate.shape[1]
    gate_up = jnp.dot(normed_two, server_mid[:, narrow:], preferred_element_type=jnp.float32)
    hidden = (jax.nn.silu(gate_up[:, :units]) * gate_up[:, units:]).astype(half_type)
    all_hidden = lax.all_gather(hidden, "mp", axis=1, tiled=True)
    product = jnp.dot(all_hidden, server_down, preferred_element_type=jnp.float32)
    own_out = (own_mixed.astype(jnp.float32) + product).astype(half_type)
    return lax.all_to_all(own_out, "mp", split_axis=0, concat_axis=1, tiled=True)


def place():
    dp_index, mp_index = lax.axis_index("dp"), lax.axis_index("mp")
    return dp_index // 2, dp_index % 2, mp_index // 2, mp_index % 2


def device(z, y, x, c):
    return (2 * z + y, 2 * x + c)


def remote(source, target, send, receive, where):
    return pltpu.make_async_remote_copy(
        src_ref=source,
        dst_ref=target,
        send_sem=send,
        recv_sem=receive,
        device_id=where,
        device_id_type=pl.DeviceIdType.MESH,
    )


def greet(peers):
    barrier = pltpu.get_barrier_semaphore()
    for peer in peers:
        pl.semaphore_signal(barrier, inc=1, device_id=peer, device_id_type=pl.DeviceIdType.MESH)
    pl.semaphore_wait(barrier, len(peers))


def plane_peers(z, y, x, c):
    return [device(z, y, 1 - x, c), device(z, 1 - y, x, c), device(z, 1 - y, 1 - x, c)]


def column_peers(z, y, x, c):
    steps = [(k, f) for k in range(4) for f in range(2) if k or f]
    return [(k, f, device((z + k) % 4, y, x, (c + f) % 2)) for k, f in steps]


class Spread:
    def __init__(self, block_ref, all_ref, send, receive, core_send, core_recv, local_sem):
        self.block, self.all, self.local_sem = block_ref, all_ref, local_sem
        self.sems = send, receive, core_send, core_recv

    def column(self, k):
        z, y, x, c = place()
        send, receive = self.sems[:2]
        where = device((z + k) % 4, y, x, c)
        return remote(self.block, self.all.at[2 * z + c], send.at[k], receive.at[k], where)

    def core(self, k):
        z, y, x, c = place()
        send, receive = self.sems[2:]
        slot = self.all.at[2 * ((z + 4 - k) % 4) + c]
        source = self.block if k == 0 else slot
        return remote(source, slot, send.at[k], receive.at[k], device(z, y, x, 1 - c))

    def own(self):
        z, y, x, c = place()
        return pltpu.make_async_copy(self.block, self.all.at[2 * z + c], self.local_sem)

    def start(self):
        for k in (1, 3, 2):
            self.column(k).start()
        self.core(0).start()
        self.own().start()

    def relay(self):
        for k in (1, 3, 2):
            self.column(k).wait_recv()
            self.core(k).start()

    def finish(self):
        self.own().wait()
        for k in (1, 3, 2):
            self.column(k).wait_send()
        for k in range(4):
            self.core(k).wait()


def regroup_kernel(
    in_ref, mid_ref, out_ref, down_ref, rows_ref,
    in_all, mid_all, out_all, down_all, rows_all,
    column_send, column_recv, plane_send, plane_recv,
    part_send, part_recv, fan_send, fan_recv, local_sem,
    rows_send, rows_recv, core_send, core_recv,
):
    z, y, x, c = place()
    own = 2 * z + y
    plane = plane_peers(z, y, x, c)
    greet([peer for _, _, peer in column_peers(z, y, x, c)] + plane)
    width = out_ref.shape[-1]

    def columns(mp):
        return pl.ds(pl.multiple_of(mp * width, width), width)

    packs = ((in_ref, in_all), (mid_ref, mid_all))
    locals_ = []
    for i, (source, target) in enumerate(packs):
        locals_.append(pltpu.make_async_copy(source.at[z], target.at[x, own], local_sem.at[i]))
    spread = Spread(rows_ref, rows_all, rows_send, rows_recv, core_send, core_recv, local_sem.at[2])
    for copy in locals_:
        copy.start()
    sends = []

    def column_copy(i, k):
        to = (z + k) % 4
        source, target = packs[i][0].at[to], packs[i][1].at[x, own]
        return remote(source, target, column_send.at[i, k], column_recv.at[i, k], device(to, y, x, c))

    halves = ((out_ref, out_all), (down_ref, down_all))
    hub = y == z // 2

    def part_copy(i, hf):
        source, target = halves[i]
        slot = (z // 2) * 2 + c
        return (
            source.at[hf],
            target.at[z // 2, :, columns(2 * x + c)],
            part_send.at[i, hf],
            part_recv.at[i, slot],
        )

    def is_self(hf):
        return (2 * y + hf == z) & (z % 2 == c)

    for k in (1, 3, 2):
        copy = column_copy(0, k)
        copy.start()
        sends.append(copy)
    for i in range(2):
        for hf in range(2):
            source, target, send, receive = part_copy(i, hf)

            @pl.when(is_self(hf))
            def _():
                pltpu.make_async_copy(source, target, receive).start()

            @pl.when(jnp.logical_not(is_self(hf)))
            def _():
                remote(source, target, send, receive, device(2 * y + hf, y, x, z % 2)).start()
    for k in (1, 3, 2):
        copy = column_copy(1, k)
        copy.start()
        sends.append(copy)

    def fan_copies(i, k):
        block = packs[i][1].at[x, 2 * ((z + 4 - k) % 4) + y]
        return [
            remote(block, block, plane_send.at[i, k, f], plane_recv.at[i, k, f], peer)
            for f, peer in enumerate(plane[:2])
        ]

    def corner_copy(i, k, half):
        zk = 2 * ((z + 4 - k) % 4)
        rows = pl.ds(half * (packs[i][1].shape[2] // 2), packs[i][1].shape[2] // 2)
        if half == 0:
            block = packs[i][1].at[1 - x, zk + y, rows]
        else:
            block = packs[i][1].at[x, zk + 1 - y, rows]
        return remote(block, block, plane_send.at[i, k, 2 + half], plane_recv.at[i, k, 2 + half], plane[1 - half])

    def corner(i):
        for k in (0, 1, 3, 2):
            for half in range(2):
                fan_copies(i, k)[half].wait_recv()
                corner_copy(i, k, half).start()

    def part_block(i, p):
        return halves[i][1].at[p // 2, :, columns(2 * x + p % 2)]

    def part_fan(i, p):
        block = part_block(i, p)
        return [
            remote(block, block, fan_send.at[i, p, f], fan_recv.at[i, p, f], peer)
            for f, peer in enumerate(plane)
        ]

    def forward(i):
        for k in (0, 1, 3, 2):
            if k == 0:
                locals_[i].wait()
            else:
                column_copy(i, k).wait_recv()
            for copy in fan_copies(i, k):
                copy.start()

    forward(0)
    spread.start()

    @pl.when(hub)
    def _():
        for i in range(2):
            for p in range(4):
                block = part_block(i, p)
                pltpu.make_async_copy(block, block, part_recv.at[i, p]).wait()
                for copy in part_fan(i, p):
                    copy.start()

    forward(1)
    corner(0)
    spread.relay()
    corner(1)
    spread.finish()
    for copy in sends:
        copy.wait_send()
    for i in range(2):
        for hf in range(2):
            source, target, send, receive = part_copy(i, hf)

            @pl.when(jnp.logical_not(is_self(hf)))
            def _():
                remote(source, target, send, receive, device(2 * y + hf, y, x, z % 2)).wait_send()
        for k in range(4):
            for half in range(2):
                fan_copies(i, k)[half].wait_send()
                corner_copy(i, k, half).wait()

    @pl.when(hub)
    def _():
        for i in range(2):
            for p in range(4):
                for copy in part_fan(i, p):
                    copy.wait_send()
                part_fan(i, p)[0].wait_recv()

    @pl.when(jnp.logical_not(hub))
    def _():
        for i in range(2):
            for p in range(4):
                for copy in part_fan(i, p)[1:]:
                    copy.wait_recv()


def any_spec():
    return pl.BlockSpec(memory_space=pl.ANY)


def regroup(*arrays):
    packed_in, packed_mid, out, down, rows = arrays
    half_type = jnp.bfloat16
    depth, cols_in = packed_in.shape[1:]
    cols_mid = packed_mid.shape[2]
    shapes = (
        (2, 8, depth, cols_in),
        (2, 8, depth, cols_mid),
        (2, out.shape[1], 4 * out.shape[2]),
        (2, down.shape[1], 4 * down.shape[2]),
        (8, *rows.shape),
    )
    dma = pltpu.SemaphoreType.DMA
    return pl.pallas_call(
        regroup_kernel,
        out_shape=[jax.ShapeDtypeStruct(shape, half_type) for shape in shapes],
        in_specs=[any_spec()] * 5,
        out_specs=[any_spec()] * 5,
        scratch_shapes=[
            dma((2, 4)), dma((2, 4)), dma((2, 4, 4)), dma((2, 4, 4)),
            dma((2, 2)), dma((2, 4)), dma((2, 4, 3)), dma((2, 4, 3)), dma((3,)),
            dma((4,)), dma((4,)), dma((4,)), dma((4,)),
        ],
        compiler_params=pltpu.CompilerParams(collective_id=0, has_side_effects=True, vmem_limit_bytes=1 << 20),
    )(*arrays)


def plane_kernel(block_ref, all_ref, send, receive, local_sem):
    z, y, x, c = place()
    peers = plane_peers(z, y, x, c)
    greet(peers)
    target = all_ref.at[2 * x + y]
    copies = [remote(block_ref, target, send.at[f], receive.at[f], p) for f, p in enumerate(peers)]
    own = pltpu.make_async_copy(block_ref, target, local_sem)
    for copy in copies:
        copy.start()
    own.start()
    own.wait()
    for copy in copies:
        copy.wait()


def plane_gather(block):
    dma = pltpu.SemaphoreType.DMA
    return pl.pallas_call(
        plane_kernel,
        out_shape=jax.ShapeDtypeStruct((4, *block.shape), block.dtype),
        in_specs=[any_spec()],
        out_specs=any_spec(),
        scratch_shapes=[dma((3,)), dma((3,)), dma(())],
        compiler_params=pltpu.CompilerParams(collective_id=1, has_side_effects=True, vmem_limit_bytes=1 << 20),
    )(block)


def near_peers(z, y, x, c):
    return [device((z + k) % 4, y, x, c) for k in (1, 2, 3)] + [device(z, y, x, 1 - c)]


def spread_kernel(block_ref, all_ref, send, receive, core_send, core_recv, local_sem):
    greet(near_peers(*place()))
    spread = Spread(block_ref, all_ref, send, receive, core_send, core_recv, local_sem)
    spread.start()
    spread.relay()
    spread.finish()


def column_gather(block):
    dma = pltpu.SemaphoreType.DMA
    return pl.pallas_call(
        spread_kernel,
        out_shape=jax.ShapeDtypeStruct((8, *block.shape), block.dtype),
        in_specs=[any_spec()],
        out_specs=any_spec(),
        scratch_shapes=[dma((4,)), dma((4,)), dma((4,)), dma((4,)), dma(())],
        compiler_params=pltpu.CompilerParams(collective_id=3, has_side_effects=True, vmem_limit_bytes=1 << 20),
    )(block)


def column_sum_kernel(parts_ref, all_ref, given, summed, core_send, core_recv, send, receive):
    z, y, x, c = place()
    greet(near_peers(z, y, x, c))
    order = (1, 3, 2, 0)

    def core(k):
        source = parts_ref.at[2 * ((z + k) % 4) + 1 - c]
        return remote(source, given.at[k], core_send.at[k], core_recv.at[k], device(z, y, x, 1 - c))

    def column(k):
        where = device((z + k) % 4, y, x, c)
        return remote(summed.at[k], all_ref.at[k], send.at[k], receive.at[k], where)

    for k in order:
        core(k).start()
    for k in order:
        core(k).wait_recv()
        both = parts_ref[2 * ((z + k) % 4) + c].astype(jnp.float32) + given[k].astype(jnp.float32)
        if k:
            summed[k] = both.astype(summed.dtype)
            column(k).start()
        else:
            all_ref[0] = both.astype(all_ref.dtype)
    for k in order:
        core(k).wait_send()
        if k:
            column(k).wait()


def column_sum(parts):
    dma = pltpu.SemaphoreType.DMA
    half = (4, *parts.shape[1:])
    vmem = pl.BlockSpec(memory_space=pltpu.VMEM)
    return pl.pallas_call(
        column_sum_kernel,
        out_shape=jax.ShapeDtypeStruct(half, parts.dtype),
        in_specs=[vmem],
        out_specs=vmem,
        scratch_shapes=[
            pltpu.VMEM(half, parts.dtype), pltpu.VMEM(half, parts.dtype),
            dma((4,)), dma((4,)), dma((4,)), dma((4,)),
        ],
        compiler_params=pltpu.CompilerParams(collective_id=2, has_side_effects=True, vmem_limit_bytes=24 << 20),
    )(parts)


def prompt_at(where, lengths):
    upto = jnp.arange(lengths.shape[0])
    ends = jnp.sum(jnp.where(upto[None, :] <= upto[:, None], lengths[None, :], 0), axis=1)
    passed = (ends[None, :] <= where[:, None]).astype(jnp.int32)
    return jnp.sum(passed, axis=1), where - jnp.sum(passed * lengths[None, :], axis=1)


def regrouped(tokens, lengths, w_query, w_key, w_value, w_out, w_gate, w_up, w_down):
    half_type = jnp.bfloat16
    z, y, x, c = place()
    rows, width = tokens.shape
    depth, narrow = w_query.shape
    units = w_gate.shape[1] // 4
    slab = rows // 4

    def pieces(weight):
        return weight.astype(half_type).reshape(weight.shape[0], 4, -1)

    packed_in = jnp.concatenate([pieces(w) for w in (w_query, w_key, w_value)], axis=2).transpose(1, 0, 2)
    packed_mid = jnp.concatenate([pieces(w) for w in (w_gate, w_up)], axis=2).transpose(1, 0, 2)
    out = w_out.astype(half_type).reshape(2, -1, narrow)
    down = w_down.astype(half_type).reshape(2, -1, narrow)
    own_rows = lax.dynamic_slice_in_dim(tokens, (2 * x + c) * slab, slab, 0)
    normed = layer_norm(own_rows).astype(half_type)
    server_in, server_mid, server_out, server_down, normed = regroup(packed_in, packed_mid, out, down, normed)
    count = 8 * slab
    normed = normed.reshape(count, width)
    server_in = server_in.reshape(2, width, 3 * HEAD)
    server_mid = server_mid.reshape(2, width, 2 * units)
    where = (
        jnp.arange(4)[:, None] * (2 * rows) + jnp.arange(2 * slab)[None, :]
    ).reshape(-1)
    q_where = where + y * rows + x * (2 * slab)
    q_prompt, q_offset = prompt_at(q_where, lengths)
    corner = jnp.arange(4)
    k_where = (((corner % 2) * rows + (corner // 2) * (2 * slab))[:, None] + where[None, :]).reshape(-1)
    k_prompt, _ = prompt_at(k_where, lengths)
    joined = [jnp.dot(normed, server_in[i], preferred_element_type=jnp.float32) for i in range(2)]
    query = rotate(jnp.stack([j[:, :HEAD] for j in joined], axis=1), q_offset).astype(half_type)
    keys = rotate(jnp.stack([j[:, HEAD : 2 * HEAD] for j in joined], axis=1), q_offset).astype(half_type)
    block = jnp.concatenate(
        [keys.reshape(count, -1)] + [j[:, 2 * HEAD :].astype(half_type) for j in joined], axis=1
    )
    pairs = plane_gather(block).reshape(4 * count, 4, HEAD)
    allowed = (q_prompt[:, None] == k_prompt[None, :]) & (k_where[None, :] <= q_where[:, None])
    scale = 1.0 / HEAD**0.5
    scores = jnp.einsum("qhd,khd->hqk", query, pairs[:, :2], preferred_element_type=jnp.float32) * scale
    scores = jnp.where(allowed[None], scores, -jnp.inf)
    weights = jnp.exp(scores - jnp.max(scores, axis=-1, keepdims=True))
    total = jnp.sum(weights, axis=-1)
    accum = jnp.einsum("hqk,khd->qhd", weights.astype(half_type), pairs[:, 2:], preferred_element_type=jnp.float32)
    context = (accum / total.T[:, :, None]).astype(half_type).reshape(count, 2 * HEAD)
    partial = jnp.dot(context, server_out.reshape(2 * HEAD, width), preferred_element_type=jnp.float32)
    shares = column_sum(partial.astype(half_type).reshape(8, slab, width))
    attended = jnp.sum(shares.astype(jnp.float32), axis=0)
    mixed = (own_rows.astype(jnp.float32) + attended).astype(half_type)
    normed_two = column_gather(layer_norm(mixed).astype(half_type)).reshape(count, width)
    hidden = []
    for i in range(2):
        gate_up = jnp.dot(normed_two, server_mid[i], preferred_element_type=jnp.float32)
        hidden.append((jax.nn.silu(gate_up[:, :units]) * gate_up[:, units:]).astype(half_type))
    hidden = jnp.concatenate(hidden, axis=1)
    product = jnp.dot(hidden, server_down.reshape(2 * units, width), preferred_element_type=jnp.float32)
    shares = column_sum(product.astype(half_type).reshape(8, slab, width))
    return (mixed.astype(jnp.float32) + jnp.sum(shares.astype(jnp.float32), axis=0)).astype(half_type)


def solution(mesh):
    in_specs = (
        P("dp", None),
        P(),
        P("dp", "mp"),
        P("dp", "mp"),
        P("dp", "mp"),
        P("dp", "mp"),
        P("dp", "mp"),
        P("dp", "mp"),
        P("dp", "mp"),
    )
    out_specs = P(("dp", "mp"), None)
    fits = mesh.shape["dp"] == 8 and mesh.shape["mp"] == 4
    return jax.shard_map(
        regrouped if fits else on_device, mesh=mesh, in_specs=in_specs, out_specs=out_specs, check_vma=False
    )
```

```python
import functools

import jax
import jax.numpy as jnp
from jax import lax
from jax.experimental import pallas as pl
from jax.experimental.pallas import tpu as pltpu
from jax.sharding import PartitionSpec as P

HEAD = 128


epsilon = 1e-05
theta_base = 10000.0


def passed_along(value, axis, steps):
    count = lax.axis_size(axis)
    initial, last = (max(0, -steps), min(count, count - steps))
    return lax.ppermute(value, axis, [(source, source + steps) for source in range(initial, last)])


def layer_norm(rows):
    values = rows.astype(jnp.float32)
    centre = jnp.mean(values, axis=-1, keepdims=True)
    spread = jnp.mean(jnp.square(values - centre), axis=-1, keepdims=True)
    return (values - centre) * lax.rsqrt(spread + epsilon)


def prompt_coords(first, count, lengths):
    where = first + jnp.arange(count)
    upto = jnp.arange(lengths.shape[0])
    ends = jnp.sum(jnp.where(upto[None, :] <= upto[:, None], lengths[None, :], 0), axis=1)
    passed = (ends[None, :] <= where[:, None]).astype(jnp.int32)
    prompt = jnp.sum(passed, axis=1)
    offset = where - jnp.sum(passed * lengths[None, :], axis=1)
    prompt = jnp.where(where < 0, -1, prompt)
    return (prompt, offset, where)


def rotate(values, offset):
    half = values.shape[-1] // 2
    freqs = jnp.power(theta_base, -jnp.arange(half, dtype=jnp.float32) * 2.0 / values.shape[-1])
    angles = offset.astype(jnp.float32)[:, None] * freqs[None, :]
    cosine = jnp.cos(angles)[:, None, :]
    sine = jnp.sin(angles)[:, None, :]
    first_half = values[..., :half]
    second_half = values[..., half:]
    return jnp.concatenate(
        [first_half * cosine - second_half * sine, second_half * cosine + first_half * sine],
        axis=-1,
    )


def on_device(tokens, lengths, w_query, w_key, w_value, w_out, w_gate, w_up, w_down):
    half_type = jnp.bfloat16
    rows = tokens.shape[0]
    narrow = w_query.shape[1]
    heads_dev = narrow // HEAD
    dp_index = lax.axis_index("dp")
    mp_index = lax.axis_index("mp")
    reach = lax.axis_size("dp") // 2
    normed = layer_norm(tokens).astype(half_type)
    packed_in = jnp.concatenate([w.astype(half_type) for w in (w_query, w_key, w_value)], axis=1)
    server_in = lax.all_gather(packed_in, "dp", axis=0, tiled=True)
    packed_mid = jnp.concatenate([w.astype(half_type) for w in (w_out, w_gate, w_up)], axis=1)
    down = w_down.astype(half_type)
    server_in, packed_mid, down = lax.optimization_barrier((server_in, packed_mid, down))
    server_mid = lax.all_gather(packed_mid, "dp", axis=0, tiled=True)
    server_mid, down = lax.optimization_barrier((server_mid, down))
    server_down = lax.all_gather(down, "dp", axis=0, tiled=True)
    joined = jnp.dot(normed, server_in, preferred_element_type=jnp.float32)
    q_prompt, q_offset, q_where = prompt_coords(dp_index * rows, rows, lengths)
    shaped = joined.reshape(rows, 3, heads_dev, HEAD)
    query = rotate(shaped[:, 0], q_offset).astype(half_type)
    keys = rotate(shaped[:, 1], q_offset).astype(half_type)
    values = shaped[:, 2].astype(half_type)
    own_first = dp_index * rows
    own_pair = jnp.stack((keys, values))
    scale = 1.0 / HEAD**0.5

    def online_step(state, pair, first):
        accum, total, top = state
        k_prompt, k_offset, k_where = prompt_coords(first, rows, lengths)
        scores = (
            jnp.einsum("qhd,khd->hqk", query, pair[0], preferred_element_type=jnp.float32) * scale
        )
        allowed = (q_prompt[:, None] == k_prompt[None, :]) & (k_where[None, :] <= q_where[:, None])
        scores = jnp.where(allowed[None], scores, -jnp.inf)
        new_top = jnp.maximum(top, jnp.max(scores, axis=-1, keepdims=True))
        fade = jnp.exp(top - new_top)
        weights = jnp.exp(scores - new_top)
        probs = weights.astype(half_type)
        product = jnp.einsum("hqk,khd->qhd", probs, pair[1], preferred_element_type=jnp.float32)
        accum = accum * jnp.transpose(fade, (1, 0, 2)) + product
        total = total * fade + jnp.sum(weights, axis=-1, keepdims=True)
        return (accum, total, new_top)

    start_state = (
        jnp.zeros((rows, heads_dev, HEAD), jnp.float32),
        jnp.zeros((heads_dev, rows, 1), jnp.float32),
        jnp.full((heads_dev, rows, 1), -jnp.inf, jnp.float32),
    )
    state = online_step(start_state, own_pair, own_first)

    def relay_step(hop, carry):
        carried, running = carry
        carried = passed_along(carried, "dp", 1)
        first = own_first - (hop + 1) * rows
        return (carried, online_step(running, carried, first))

    unused, state = lax.fori_loop(0, reach, relay_step, (own_pair, state))
    accum, total, top = state
    context = (accum / jnp.transpose(total, (1, 0, 2))).astype(half_type).reshape(rows, narrow)
    all_heads = lax.all_gather(context, "mp", axis=1, tiled=True)
    attended = jnp.dot(all_heads, server_mid[:, :narrow], preferred_element_type=jnp.float32)
    own_columns = lax.dynamic_slice_in_dim(tokens, mp_index * narrow, narrow, 1)
    own_mixed = (own_columns.astype(jnp.float32) + attended).astype(half_type)
    mixed = lax.all_gather(own_mixed, "mp", axis=1, tiled=True)
    normed_two = layer_norm(mixed).astype(half_type)
    units = w_gate.shape[1]
    gate_up = jnp.dot(normed_two, server_mid[:, narrow:], preferred_element_type=jnp.float32)
    hidden = (jax.nn.silu(gate_up[:, :units]) * gate_up[:, units:]).astype(half_type)
    all_hidden = lax.all_gather(hidden, "mp", axis=1, tiled=True)
    product = jnp.dot(all_hidden, server_down, preferred_element_type=jnp.float32)
    own_out = (own_mixed.astype(jnp.float32) + product).astype(half_type)
    return lax.all_to_all(own_out, "mp", split_axis=0, concat_axis=1, tiled=True)


def place():
    dp_index, mp_index = lax.axis_index("dp"), lax.axis_index("mp")
    return dp_index // 2, dp_index % 2, mp_index // 2, mp_index % 2


def device(z, y, x, c):
    return (2 * z + y, 2 * x + c)


def remote(source, target, send, receive, where):
    return pltpu.make_async_remote_copy(
        src_ref=source,
        dst_ref=target,
        send_sem=send,
        recv_sem=receive,
        device_id=where,
        device_id_type=pl.DeviceIdType.MESH,
    )


def greet(peers):
    barrier = pltpu.get_barrier_semaphore()
    for peer in peers:
        pl.semaphore_signal(barrier, inc=1, device_id=peer, device_id_type=pl.DeviceIdType.MESH)
    pl.semaphore_wait(barrier, len(peers))


def plane_peers(z, y, x, c):
    return [device(z, y, 1 - x, c), device(z, 1 - y, x, c), device(z, 1 - y, 1 - x, c)]


def column_peers(z, y, x, c):
    steps = [(k, f) for k in range(4) for f in range(2) if k or f]
    return [(k, f, device((z + k) % 4, y, x, (c + f) % 2)) for k, f in steps]


class Spread:
    def __init__(self, block_ref, all_ref, send, receive, core_send, core_recv, local_sem):
        self.block, self.all, self.local_sem = block_ref, all_ref, local_sem
        self.sems = send, receive, core_send, core_recv

    def column(self, k):
        z, y, x, c = place()
        send, receive = self.sems[:2]
        where = device((z + k) % 4, y, x, c)
        return remote(self.block, self.all.at[2 * z + c], send.at[k], receive.at[k], where)

    def core(self, k):
        z, y, x, c = place()
        send, receive = self.sems[2:]
        slot = self.all.at[2 * ((z + 4 - k) % 4) + c]
        source = self.block if k == 0 else slot
        return remote(source, slot, send.at[k], receive.at[k], device(z, y, x, 1 - c))

    def own(self):
        z, y, x, c = place()
        return pltpu.make_async_copy(self.block, self.all.at[2 * z + c], self.local_sem)

    def start(self):
        for k in (1, 3, 2):
            self.column(k).start()
        self.core(0).start()
        self.own().start()

    def relay(self):
        for k in (1, 3, 2):
            self.column(k).wait_recv()
            self.core(k).start()

    def finish(self):
        self.own().wait()
        for k in (1, 3, 2):
            self.column(k).wait_send()
        for k in range(4):
            self.core(k).wait()


def regroup_kernel(
    in_ref, mid_ref, out_ref, down_ref, rows_ref,
    in_all, mid_all, out_all, down_all, rows_all,
    column_send, column_recv, plane_send, plane_recv,
    part_send, part_recv, fan_send, fan_recv, local_sem,
    rows_send, rows_recv, core_send, core_recv,
):
    z, y, x, c = place()
    own = 2 * z + y
    plane = plane_peers(z, y, x, c)
    greet([peer for _, _, peer in column_peers(z, y, x, c)] + plane)
    width = out_ref.shape[-1]

    def columns(mp):
        return pl.ds(pl.multiple_of(mp * width, width), width)

    packs = ((in_ref, in_all), (mid_ref, mid_all))
    locals_ = []
    for i, (source, target) in enumerate(packs):
        locals_.append(pltpu.make_async_copy(source.at[z], target.at[x, own] if i == 0 else target.at[z], local_sem.at[i]))
    spread = Spread(rows_ref, rows_all, rows_send, rows_recv, core_send, core_recv, local_sem.at[2])
    for copy in locals_:
        copy.start()
    sends = []

    def column_copy(i, k):
        to = (z + k) % 4
        source = packs[i][0].at[to]
        target = packs[i][1].at[x, own] if i == 0 else packs[i][1].at[z]
        return remote(source, target, column_send.at[i, k], column_recv.at[i, k], device(to, y, x, c))

    halves = ((out_ref, out_all), (down_ref, down_all))
    hub = y == z // 2

    def part_copy(i, hf):
        source, target = halves[i]
        slot = (z // 2) * 2 + c
        return (
            source.at[hf],
            target.at[z // 2, :, columns(2 * x + c)],
            part_send.at[i, hf],
            part_recv.at[i, slot],
        )

    def is_self(hf):
        return (2 * y + hf == z) & (z % 2 == c)

    for k in (1, 3, 2):
        copy = column_copy(0, k)
        copy.start()
        sends.append(copy)
    for i in range(2):
        for hf in range(2):
            source, target, send, receive = part_copy(i, hf)

            @pl.when(is_self(hf))
            def _():
                pltpu.make_async_copy(source, target, receive).start()

            @pl.when(jnp.logical_not(is_self(hf)))
            def _():
                remote(source, target, send, receive, device(2 * y + hf, y, x, z % 2)).start()
    for k in (1, 3, 2):
        copy = column_copy(1, k)
        copy.start()
        sends.append(copy)

    def fan_copies(i, k):
        block = packs[i][1].at[x, 2 * ((z + 4 - k) % 4) + y]
        return [
            remote(block, block, plane_send.at[i, k, f], plane_recv.at[i, k, f], peer)
            for f, peer in enumerate(plane[:2])
        ]

    def corner_copy(i, k, half):
        zk = 2 * ((z + 4 - k) % 4)
        rows = pl.ds(half * (packs[i][1].shape[2] // 2), packs[i][1].shape[2] // 2)
        if half == 0:
            block = packs[i][1].at[1 - x, zk + y, rows]
        else:
            block = packs[i][1].at[x, zk + 1 - y, rows]
        return remote(block, block, plane_send.at[i, k, 2 + half], plane_recv.at[i, k, 2 + half], plane[1 - half])

    def corner(i):
        for k in (0, 1, 3, 2):
            for half in range(2):
                fan_copies(i, k)[half].wait_recv()
                corner_copy(i, k, half).start()

    def part_block(i, p):
        return halves[i][1].at[p // 2, :, columns(2 * x + p % 2)]

    def part_fan(i, p):
        block = part_block(i, p)
        return [
            remote(block, block, fan_send.at[i, p, f], fan_recv.at[i, p, f], peer)
            for f, peer in enumerate(plane)
        ]

    def forward(i):
        for k in (0, 1, 3, 2):
            if k == 0:
                locals_[i].wait()
            else:
                column_copy(i, k).wait_recv()
            for copy in fan_copies(i, k):
                copy.start()

    forward(0)
    spread.start()

    @pl.when(hub)
    def _():
        for i in range(2):
            for p in range(4):
                block = part_block(i, p)
                pltpu.make_async_copy(block, block, part_recv.at[i, p]).wait()
                for copy in part_fan(i, p):
                    copy.start()

    corner(0)
    spread.relay()
    locals_[1].wait()
    for k in (1, 3, 2):
        column_copy(1, k).wait_recv()
    spread.finish()
    for copy in sends:
        copy.wait_send()
    for i in range(2):
        for hf in range(2):
            source, target, send, receive = part_copy(i, hf)

            @pl.when(jnp.logical_not(is_self(hf)))
            def _():
                remote(source, target, send, receive, device(2 * y + hf, y, x, z % 2)).wait_send()
    for k in range(4):
        for half in range(2):
            fan_copies(0, k)[half].wait_send()
            corner_copy(0, k, half).wait()

    @pl.when(hub)
    def _():
        for i in range(2):
            for p in range(4):
                for copy in part_fan(i, p):
                    copy.wait_send()
                part_fan(i, p)[0].wait_recv()

    @pl.when(jnp.logical_not(hub))
    def _():
        for i in range(2):
            for p in range(4):
                for copy in part_fan(i, p)[1:]:
                    copy.wait_recv()


def any_spec():
    return pl.BlockSpec(memory_space=pl.ANY)


def regroup(*arrays):
    packed_in, packed_mid, out, down, rows = arrays
    half_type = jnp.bfloat16
    depth, cols_in = packed_in.shape[1:]
    cols_mid = packed_mid.shape[2]
    shapes = (
        (2, 8, depth, cols_in),
        (4, depth, cols_mid),
        (2, out.shape[1], 4 * out.shape[2]),
        (2, down.shape[1], 4 * down.shape[2]),
        (8, *rows.shape),
    )
    dma = pltpu.SemaphoreType.DMA
    return pl.pallas_call(
        regroup_kernel,
        out_shape=[jax.ShapeDtypeStruct(shape, half_type) for shape in shapes],
        in_specs=[any_spec()] * 5,
        out_specs=[any_spec()] * 5,
        scratch_shapes=[
            dma((2, 4)), dma((2, 4)), dma((2, 4, 4)), dma((2, 4, 4)),
            dma((2, 2)), dma((2, 4)), dma((2, 4, 3)), dma((2, 4, 3)), dma((3,)),
            dma((4,)), dma((4,)), dma((4,)), dma((4,)),
        ],
        compiler_params=pltpu.CompilerParams(collective_id=0, has_side_effects=True, vmem_limit_bytes=1 << 20),
    )(*arrays)


def plane_kernel(block_ref, all_ref, send, receive, local_sem):
    z, y, x, c = place()
    peers = plane_peers(z, y, x, c)
    greet(peers)
    target = all_ref.at[2 * x + y]
    copies = [remote(block_ref, target, send.at[f], receive.at[f], p) for f, p in enumerate(peers)]
    own = pltpu.make_async_copy(block_ref, target, local_sem)
    for copy in copies:
        copy.start()
    own.start()
    own.wait()
    for copy in copies:
        copy.wait()


def plane_gather(block):
    dma = pltpu.SemaphoreType.DMA
    return pl.pallas_call(
        plane_kernel,
        out_shape=jax.ShapeDtypeStruct((4, *block.shape), block.dtype),
        in_specs=[any_spec()],
        out_specs=any_spec(),
        scratch_shapes=[dma((3,)), dma((3,)), dma(())],
        compiler_params=pltpu.CompilerParams(collective_id=1, has_side_effects=True, vmem_limit_bytes=1 << 20),
    )(block)


def near_peers(z, y, x, c):
    return [device((z + k) % 4, y, x, c) for k in (1, 2, 3)] + [device(z, y, x, 1 - c)]


def spread_kernel(
    block_ref, mid_ref, all_ref, mid_all,
    send, receive, core_send, core_recv, local_sem, mid_send, mid_recv, mid_sem,
):
    z, y, x, c = place()
    plane = plane_peers(z, y, x, c)
    greet(near_peers(z, y, x, c) + plane)
    own = [pltpu.make_async_copy(mid_ref.at[k], mid_all.at[x, k, y], mid_sem.at[k]) for k in range(4)]
    copies = [
        remote(mid_ref.at[k], mid_all.at[x, k, y], mid_send.at[k, f], mid_recv.at[k, f], peer)
        for k in range(4)
        for f, peer in enumerate(plane)
    ]
    spread = Spread(block_ref, all_ref, send, receive, core_send, core_recv, local_sem)
    spread.start()
    for copy in copies + own:
        copy.start()
    spread.relay()
    spread.finish()
    for copy in copies + own:
        copy.wait()


def column_gather(block, mid):
    dma = pltpu.SemaphoreType.DMA
    return pl.pallas_call(
        spread_kernel,
        out_shape=[
            jax.ShapeDtypeStruct((8, *block.shape), block.dtype),
            jax.ShapeDtypeStruct((2, 4, 2, *mid.shape[1:]), mid.dtype),
        ],
        in_specs=[any_spec()] * 2,
        out_specs=[any_spec()] * 2,
        scratch_shapes=[
            dma((4,)), dma((4,)), dma((4,)), dma((4,)), dma(()),
            dma((4, 3)), dma((4, 3)), dma((4,)),
        ],
        compiler_params=pltpu.CompilerParams(collective_id=3, has_side_effects=True, vmem_limit_bytes=1 << 20),
    )(block, mid)


def column_sum_kernel(parts_ref, all_ref, given, summed, core_send, core_recv, send, receive):
    z, y, x, c = place()
    greet(near_peers(z, y, x, c))
    order = (1, 3, 2, 0)

    def core(k):
        source = parts_ref.at[2 * ((z + k) % 4) + 1 - c]
        return remote(source, given.at[k], core_send.at[k], core_recv.at[k], device(z, y, x, 1 - c))

    def column(k):
        where = device((z + k) % 4, y, x, c)
        return remote(summed.at[k], all_ref.at[k], send.at[k], receive.at[k], where)

    for k in order:
        core(k).start()
    for k in order:
        core(k).wait_recv()
        both = parts_ref[2 * ((z + k) % 4) + c].astype(jnp.float32) + given[k].astype(jnp.float32)
        if k:
            summed[k] = both.astype(summed.dtype)
            column(k).start()
        else:
            all_ref[0] = both.astype(all_ref.dtype)
    for k in order:
        core(k).wait_send()
        if k:
            column(k).wait()


def column_sum(parts):
    dma = pltpu.SemaphoreType.DMA
    half = (4, *parts.shape[1:])
    vmem = pl.BlockSpec(memory_space=pltpu.VMEM)
    return pl.pallas_call(
        column_sum_kernel,
        out_shape=jax.ShapeDtypeStruct(half, parts.dtype),
        in_specs=[vmem],
        out_specs=vmem,
        scratch_shapes=[
            pltpu.VMEM(half, parts.dtype), pltpu.VMEM(half, parts.dtype),
            dma((4,)), dma((4,)), dma((4,)), dma((4,)),
        ],
        compiler_params=pltpu.CompilerParams(collective_id=2, has_side_effects=True, vmem_limit_bytes=24 << 20),
    )(parts)


def prompt_at(where, lengths):
    upto = jnp.arange(lengths.shape[0])
    ends = jnp.sum(jnp.where(upto[None, :] <= upto[:, None], lengths[None, :], 0), axis=1)
    passed = (ends[None, :] <= where[:, None]).astype(jnp.int32)
    return jnp.sum(passed, axis=1), where - jnp.sum(passed * lengths[None, :], axis=1)


def regrouped(tokens, lengths, w_query, w_key, w_value, w_out, w_gate, w_up, w_down):
    half_type = jnp.bfloat16
    z, y, x, c = place()
    rows, width = tokens.shape
    depth, narrow = w_query.shape
    units = w_gate.shape[1] // 4
    slab = rows // 4

    def pieces(weight):
        return weight.astype(half_type).reshape(weight.shape[0], 4, -1)

    packed_in = jnp.concatenate([pieces(w) for w in (w_query, w_key, w_value)], axis=2).transpose(1, 0, 2)
    packed_mid = jnp.concatenate([pieces(w) for w in (w_gate, w_up)], axis=2).transpose(1, 0, 2)
    out = w_out.astype(half_type).reshape(2, -1, narrow)
    down = w_down.astype(half_type).reshape(2, -1, narrow)
    own_rows = lax.dynamic_slice_in_dim(tokens, (2 * x + c) * slab, slab, 0)
    normed = layer_norm(own_rows).astype(half_type)
    server_in, server_mid, server_out, server_down, normed = regroup(packed_in, packed_mid, out, down, normed)
    count = 8 * slab
    normed = normed.reshape(count, width)
    server_in = server_in.reshape(2, width, 3 * HEAD)
    where = (
        jnp.arange(4)[:, None] * (2 * rows) + jnp.arange(2 * slab)[None, :]
    ).reshape(-1)
    q_where = where + y * rows + x * (2 * slab)
    q_prompt, q_offset = prompt_at(q_where, lengths)
    corner = jnp.arange(4)
    k_where = (((corner % 2) * rows + (corner // 2) * (2 * slab))[:, None] + where[None, :]).reshape(-1)
    k_prompt, _ = prompt_at(k_where, lengths)
    joined = [jnp.dot(normed, server_in[i], preferred_element_type=jnp.float32) for i in range(2)]
    query = rotate(jnp.stack([j[:, :HEAD] for j in joined], axis=1), q_offset).astype(half_type)
    keys = rotate(jnp.stack([j[:, HEAD : 2 * HEAD] for j in joined], axis=1), q_offset).astype(half_type)
    block = jnp.concatenate(
        [keys.reshape(count, -1)] + [j[:, 2 * HEAD :].astype(half_type) for j in joined], axis=1
    )
    pairs = plane_gather(block).reshape(4 * count, 4, HEAD)
    allowed = (q_prompt[:, None] == k_prompt[None, :]) & (k_where[None, :] <= q_where[:, None])
    scale = 1.0 / HEAD**0.5
    scores = jnp.einsum("qhd,khd->hqk", query, pairs[:, :2], preferred_element_type=jnp.float32) * scale
    scores = jnp.where(allowed[None], scores, -jnp.inf)
    weights = jnp.exp(scores - jnp.max(scores, axis=-1, keepdims=True))
    total = jnp.sum(weights, axis=-1)
    accum = jnp.einsum("hqk,khd->qhd", weights.astype(half_type), pairs[:, 2:], preferred_element_type=jnp.float32)
    context = (accum / total.T[:, :, None]).astype(half_type).reshape(count, 2 * HEAD)
    partial = jnp.dot(context, server_out.reshape(2 * HEAD, width), preferred_element_type=jnp.float32)
    shares = column_sum(partial.astype(half_type).reshape(8, slab, width))
    attended = jnp.sum(shares.astype(jnp.float32), axis=0)
    mixed = (own_rows.astype(jnp.float32) + attended).astype(half_type)
    normed_two, server_mid = column_gather(layer_norm(mixed).astype(half_type), server_mid)
    normed_two = normed_two.reshape(count, width)
    server_mid = server_mid.reshape(2, width, 2 * units)
    hidden = []
    for i in range(2):
        gate_up = jnp.dot(normed_two, server_mid[i], preferred_element_type=jnp.float32)
        hidden.append((jax.nn.silu(gate_up[:, :units]) * gate_up[:, units:]).astype(half_type))
    hidden = jnp.concatenate(hidden, axis=1)
    product = jnp.dot(hidden, server_down.reshape(2 * units, width), preferred_element_type=jnp.float32)
    shares = column_sum(product.astype(half_type).reshape(8, slab, width))
    return (mixed.astype(jnp.float32) + jnp.sum(shares.astype(jnp.float32), axis=0)).astype(half_type)


def solution(mesh):
    in_specs = (
        P("dp", None),
        P(),
        P("dp", "mp"),
        P("dp", "mp"),
        P("dp", "mp"),
        P("dp", "mp"),
        P("dp", "mp"),
        P("dp", "mp"),
        P("dp", "mp"),
    )
    out_specs = P(("dp", "mp"), None)
    fits = mesh.shape["dp"] == 8 and mesh.shape["mp"] == 4
    return jax.shard_map(
        regrouped if fits else on_device, mesh=mesh, in_specs=in_specs, out_specs=out_specs, check_vma=False
    )
```
